256 devices in a mesh: row: 4 (over x), col: 4 (over z_lo), rep: 16 (over z_hi, y, core).
Axes of the slice: x: 4, y: 4, z: 8 (z_hi: 2, z_lo: 4; z = z_hi * 4 + z_lo), core: 2. Of those that a mesh axis runs over, the one named last changes fastest.
Arguments:
- integrals: bfloat16 [8192, 32768], P('row', ('col', 'rep')), may hold values from -0.0625 to 0.0625
- amplitudes: bfloat16 [32768, 4096], P(('row', 'rep'), 'col'), may hold values from -6 to 6
- tile_cols: int32 [64, 64], P('row'), may hold values from 0 to 255, as said below
Outputs:
- ladder: bfloat16 [8192, 4096], P(('row', 'rep'), 'col')
The draws below stay inside these ranges and needn't reach their ends.
Inputs may be any that keep to these rules, and one draw needn't show every extreme that they name: `tile_cols`: tile columns are split into aligned groups of 4; entries g * 1 to (g + 1) - 1 of a tile row are 1 distinct tile columns of group g, in increasing order.
All inputs are finite; a program needn't handle non-finite values.
Results may differ from the reference program's by a relative error of at most 0.001.
Values may be sent and summed in bfloat16 or wider, within the bound.
A program may use at most 64 MiB of HBM per device.

```python
import jax
import jax.numpy as jnp
from jax import lax

TILE = 128
K_DEV = 512
M = 8192
K = 32768
N = 4096
MB = 64
KB = 256
NNZ = 64


def draw_tile_cols(key, part):
    key = jax.random.fold_in(key, 11)
    block_tiles = K_DEV // TILE
    kept_tiles = block_tiles // 4
    groups = KB // block_tiles
    scores = jax.random.randint(key, (MB, groups, block_tiles), 0, 1 << 20) * block_tiles
    scores = scores + jnp.arange(block_tiles, dtype=jnp.int32)[None, None, :]
    order = jnp.argsort(scores, axis=-1, stable=True)[:, :, :kept_tiles]
    chosen = jnp.sort(order, axis=-1).astype(jnp.int32)
    offsets = (jnp.arange(groups, dtype=jnp.int32) * block_tiles)[None, :, None]
    return (chosen + offsets).reshape(MB, NNZ).astype(jnp.int32)


def level_of(own_key, extent, split, least, high):
    loudness = 1.0
    for dim, shards_of in split:
        steps = jax.random.uniform(jax.random.fold_in(jax.random.fold_in(own_key, 6), dim), (shards_of,), jnp.float32, least / len(split), high / len(split))
        loudness = loudness * jnp.repeat(jnp.exp(steps), extent[dim] // shards_of).reshape((-1,) + (1,) * (len(extent) - 1 - dim))
    return loudness


def bell_draw(stream_key, extent, width, bound, shards=(), kind=jnp.bfloat16):
    array = jax.random.normal(stream_key, extent, jnp.float32) * width
    if len(shards) > 0:
        array = level_of(stream_key, extent, shards, -0.22, 0.18) * array
    return jnp.clip(array, min=-bound, max=bound).astype(kind)


def setup_inputs(seed: int = 0) -> dict:
    splits = jax.random.split(jax.random.key(seed), 4)
    return {
        "integrals": bell_draw(splits[0], (M, K), (NNZ * TILE) ** -0.5, 0.0625, ((0, 4), (1, 64))),
        "amplitudes": bell_draw(splits[1], (K, N), 1.0, 6.0, ((0, 64), (1, 4))),
        "tile_cols": draw_tile_cols(jax.random.fold_in(splits[3], 71), 0),
    }


def reference(integrals, amplitudes, tile_cols):
    tiled_amps = amplitudes.reshape(KB, TILE, N)
    row_tiles = integrals.reshape(MB, TILE, KB, TILE)

    def one_row(index):
        chosen_cols = tile_cols[index]
        block = row_tiles[index][:, chosen_cols, :].reshape(TILE, NNZ * TILE)
        rows_b = tiled_amps[chosen_cols].reshape(NNZ * TILE, N)
        return jnp.dot(block, rows_b, preferred_element_type=jnp.float32).astype(jnp.bfloat16)

    result = lax.map(one_row, jnp.arange(MB, dtype=jnp.int32))
    return result.reshape(M, N)
```

```python
import jax
import jax.numpy as jnp
from jax import lax
from jax.experimental import pallas as pl
from jax.experimental.pallas import tpu as pltpu
from jax.sharding import PartitionSpec as P

TILE = 128
MESH = pl.DeviceIdType.MESH
BF16 = jnp.bfloat16
F32 = jnp.float32

NQ = 8
NC = 2 * NQ
AHEAD = 3
LAG_DOT = 2
LAG_CORE = 3
LAG_Y1 = 5
LAG_Y2 = 7


def choose(j, tiles):
    low = jnp.where(j == 0, tiles[0], tiles[1])
    high = jnp.where(j == 2, tiles[2], tiles[3])
    return jnp.where(j < 2, low, high)


def kernel(integrals, amplitudes, tile_cols, out,
           raw0, raw1, ints, a0, a1, a2, a3, a4, a5, a6, a7, keep, give, got, y1, y2, zgot,
           load_a, load_i, a_send, a_recv, af_send, af_recv,
           i_send, i_recv, if_send, c_send, c_recv,
           y1_send, y1_recv, y2_send, y2_recv, z_send, z_recv):
    x = lax.axis_index("row")
    zl = lax.axis_index("col")
    p = lax.axis_index("rep")
    zh = p // 8
    y = lax.rem(p // 2, 4)
    core = lax.rem(p, 2)
    z = zh * 4 + zl
    xr, xl = lax.rem(x + 1, 4), lax.rem(x + 3, 4)
    yr, yl, yo = lax.rem(y + 1, 4), lax.rem(y + 3, 4), lax.rem(y + 2, 4)

    def at_x(v):
        return (v, zl, p)

    def at_y(v):
        return (x, zl, zh * 8 + v * 2 + core)

    def at_z(v):
        v = lax.rem(v + 8, 8)
        return (x, lax.rem(v, 4), (v // 4) * 8 + y * 2 + core)

    other_core = (x, zl, zh * 8 + y * 2 + (1 - core))

    def remote(src, dst, send, recv, dev):
        return pltpu.make_async_remote_copy(
            src_ref=src, dst_ref=dst, send_sem=send, recv_sem=recv,
            device_id=dev, device_id_type=MESH)

    def half(m):
        return (1 - zh) * (1 - m) + zh * m

    raw = (raw0, raw1)
    amps = (a0, a1, a2, a3, a4, a5, a6, a7)

    def i_load(m):
        rows = pl.ds(pl.multiple_of(half(m) * 1024, 1024), 1024)
        return pltpu.make_async_copy(integrals.at[rows], raw[m], load_i.at[m])

    for m in range(2):
        i_load(m).start()

    def a_load(q):
        cols = pl.ds(pl.multiple_of(q * TILE, TILE), TILE)
        return pltpu.make_async_copy(amplitudes.at[:, cols], amps[q].at[x], load_a.at[q])

    for q in range(NQ):
        a_load(q).start()

    barrier = pltpu.get_barrier_semaphore()
    partners = [at_x(xr), at_x(xl), at_y(yr), at_y(yl), at_z(z + 1), at_z(z - 1),
                at_z(z + 2), at_z(z - 2), at_z(z + 4), other_core]
    for dev in partners:
        pl.semaphore_signal(barrier, inc=1, device_id=dev, device_id_type=MESH)

    def pack(m):
        i_load(m).wait()
        group = zl * 16 + p
        for k in range(8):
            i = half(m) * 8 + k
            j = tile_cols[i, group] - group * 4
            rows = pl.ds(k * TILE, TILE)
            ints[zl, i] = choose(j, [raw[m][rows, pl.ds(n * TILE, TILE)] for n in range(4)])

    def i_copy(m, h, send, target):
        part = ints.at[h, pl.ds(half(m) * 8, 8)]
        return remote(part, part, send, i_recv.at[m, h], at_z(zh * 4 + target))

    steps = ((0, 2), (1, -2), (2, 1), (3, -1))

    def i_own(m, wait):
        for s, d in steps:
            @pl.when((zl + d >= 0) & (zl + d < 4))
            def _():
                copy = i_copy(m, zl, i_send.at[m, s], zl + d)
                if wait:
                    copy.wait_send()
                else:
                    copy.start()

    def i_forward(m, wait):
        @pl.when((zl == 1) | (zl == 2))
        def _():
            h = jnp.where(zl == 2, 0, 3)
            copy = i_copy(m, h, if_send.at[m], jnp.where(zl == 2, 3, 0))
            if wait:
                copy.wait_send()
            else:
                copy.wait_recv()
                copy.start()

    def i_arrive(m):
        for d in range(1, 4):
            h = lax.rem(zl + d, 4)

            @pl.when(jnp.logical_not(((zl == 2) & (h == 0)) | ((zl == 1) & (h == 3))))
            def _():
                i_copy(m, h, if_send.at[m], zl).wait_recv()

    def a_own(q, d):
        part = amps[q].at[x]
        return remote(part, part, a_send.at[q, d], a_recv.at[q, d], at_x((xr, xl)[d]))

    def a_from(q, d):
        part = amps[q].at[(xl, xr)[d]]
        return remote(part, part, a_send.at[q, d], a_recv.at[q, d], at_x((xr, xl)[d]))

    def a_pass(q, d):
        part = amps[q].at[(xl, xr)[d], pl.ds(d * 256, 256)]
        return remote(part, part, af_send.at[q, d], af_recv.at[q, d], at_x((xr, xl)[d]))

    def a_passed(q, d):
        part = amps[q].at[lax.rem(x + 2, 4), pl.ds(d * 256, 256)]
        return remote(part, part, af_send.at[q, d], af_recv.at[q, d], at_x((xr, xl)[d]))

    def a_start(q):
        a_load(q).wait()
        for d in range(2):
            a_own(q, d).start()

    pack(0)
    pl.semaphore_wait(barrier, len(partners))
    i_own(0, False)
    for q in range(AHEAD):
        a_start(q)
    pack(1)
    i_own(1, False)

    def product(c, m, q, cc, dst):
        def row(yy, carry):
            i = half(m) * 8 + yy * 2 + cc
            lhs, rhs = [], []
            for h in range(4):
                group = h * 16 + p
                j = tile_cols[i, group] - group * 4
                lhs.append(ints[h, i])
                rhs.append(choose(j, [amps[q][h, pl.ds(n * TILE, TILE)] for n in range(4)]))
            dst[c, yy] = jnp.dot(jnp.concatenate(lhs, axis=1), jnp.concatenate(rhs, axis=0),
                                 preferred_element_type=F32)
            return carry
        lax.fori_loop(0, 4, row, 0)

    def core_copy(c):
        return remote(give.at[c], got.at[c], c_send, c_recv.at[c], other_core)

    def y1_copy(c, d):
        return remote(keep.at[c, yo, pl.ds(d * 64, 64)], y1.at[c, d], y1_send, y1_recv.at[c, d],
                      at_y((yr, yl)[d]))

    def y2_copy(c, d):
        return remote(keep.at[c, (yr, yl)[d]], y2.at[c, d], y2_send, y2_recv.at[c, d],
                      at_y((yr, yl)[d]))

    def z_copy(q):
        return remote(keep.at[q, y], zgot.at[q], z_send, z_recv.at[q], at_z(z + 4))

    def tick(t, carry):
        for q in range(NQ):
            @pl.when(t == q)
            def _():
                for d in range(2):
                    a_from(q, d).wait_recv()
                    a_pass(q, d).start()
                if q + AHEAD < NQ:
                    a_start(q + AHEAD)

        @pl.when(t == 1)
        def _():
            i_forward(0, False)

        @pl.when(t == 4)
        def _():
            i_forward(1, False)

        c = t - LAG_DOT

        @pl.when(c == 0)
        def _():
            i_arrive(0)

        @pl.when(c == NQ)
        def _():
            i_arrive(1)

        m = c // NQ
        for q in range(NQ):
            @pl.when(c == q)
            def _():
                for d in range(2):
                    a_passed(q, d).wait_recv()

            @pl.when((c == q) | (c == q + NQ))
            def _():
                product(c, m, q, 1 - core, give)
                core_copy(c).start()
                product(c, m, q, core, keep)

        c1 = t - LAG_CORE

        @pl.when((c1 >= 0) & (c1 < NC))
        def _():
            core_copy(c1).wait_recv()
            keep[c1, yo] += got[c1, yo]
            for d in range(2):
                y1_copy(c1, d).start()
            for v in (yr, yl, y):
                keep[c1, v] += got[c1, v]

        c2 = t - LAG_Y1

        @pl.when((c2 >= 0) & (c2 < NC))
        def _():
            for d in range(2):
                y1_copy(c2, d).wait_recv()
                keep[c2, (yr, yl)[d], pl.ds(d * 64, 64)] += y1[c2, d]
                y2_copy(c2, d).start()

        c3 = t - LAG_Y2

        @pl.when((c3 >= 0) & (c3 < NC))
        def _():
            for d in range(2):
                y2_copy(c3, d).wait_recv()

            @pl.when(c3 < NQ)
            def _():
                keep[c3, y] += y2[c3, 0] + y2[c3, 1]
                z_copy(c3).start()

            @pl.when(c3 >= NQ)
            def _():
                q = c3 - NQ
                z_copy(q).wait_recv()
                total = (keep[c3, y] + y2[c3, 0]) + (y2[c3, 1] + zgot[q])
                out[:, pl.ds(pl.multiple_of(q * TILE, TILE), TILE)] = total.astype(BF16)

        return carry

    lax.fori_loop(0, NC + LAG_Y2, tick, 0)

    for m in range(2):
        i_own(m, True)
        i_forward(m, True)
    for d in range(2):
        for q in range(NQ):
            a_own(q, d).wait_send()
            a_pass(q, d).wait_send()
    for buf, sem in ((give, c_send), (y1, y1_send), (y2, y2_send), (zgot, z_send)):
        remote(buf, buf, sem, c_recv.at[0], other_core).wait_send()


def body(integrals, amplitudes, tile_cols):
    dma = pltpu.SemaphoreType.DMA
    return pl.pallas_call(
        kernel,
        out_shape=jax.ShapeDtypeStruct((TILE, 1024), BF16),
        in_specs=[pl.BlockSpec(memory_space=pl.ANY), pl.BlockSpec(memory_space=pl.ANY),
                  pl.BlockSpec(memory_space=pltpu.SMEM)],
        out_specs=pl.BlockSpec(memory_space=pltpu.VMEM),
        scratch_shapes=[
            *[pltpu.VMEM((1024, 512), BF16)] * 2,
            pltpu.VMEM((4, 16, TILE, TILE), BF16),
            *[pltpu.VMEM((4, 512, TILE), BF16)] * NQ,
            pltpu.VMEM((NC, 4, TILE, TILE), F32),
            pltpu.VMEM((NC, 4, TILE, TILE), F32),
            pltpu.VMEM((NC, 4, TILE, TILE), F32),
            pltpu.VMEM((NC, 2, 64, TILE), F32),
            pltpu.VMEM((NC, 2, TILE, TILE), F32),
            pltpu.VMEM((NQ, TILE, TILE), F32),
            dma((NQ,)), dma((2,)), *[dma((NQ, 2))] * 4,
            dma((2, 4)), dma((2, 4)), dma((2,)), dma, dma((NC,)),
            dma, dma((NC, 2)), dma, dma((NC, 2)), dma, dma((NQ,)),
        ],
        compiler_params=pltpu.CompilerParams(
            collective_id=0, has_side_effects=True, vmem_limit_bytes=48 << 20),
        cost_estimate=pl.CostEstimate(flops=2 << 30, bytes_accessed=4 << 20, transcendentals=0),
    )(integrals, amplitudes, tile_cols)


def solution(mesh):
    return jax.shard_map(
        body,
        mesh=mesh,
        in_specs=(P("row", ("col", "rep")), P(("row", "rep"), "col"), P("row", None)),
        out_specs=P(("row", "rep"), "col"),
        check_vma=False,
    )
```

```python
import jax
import jax.numpy as jnp
from jax import lax
from jax.experimental import pallas as pl
from jax.experimental.pallas import tpu as pltpu
from jax.sharding import PartitionSpec as P

TILE = 128
MESH = pl.DeviceIdType.MESH
BF16 = jnp.bfloat16
F32 = jnp.float32

NQ = 8
HALF = 64
WIDE = 256
ORDER = ((0, 0), (0, 1), (1, 0), (1, 1), (2, 0), (2, 1), (0, 2), (1, 2),
         (2, 2), (0, 3), (1, 3), (2, 3), (3, 0), (3, 1), (3, 2), (3, 3))
NC = len(ORDER)
A_TICK = (0, 1, 2, 3, 5, 6, 9, 11)
I_TICK = (1, 4, 7, 10)
C_TICK = (4, 7, 8, 9, 10, 11, 12, 13, 14, 15, 16, 17, 18, 19, 20, 21)
AHEAD = 3
LAG_CORE = 1
LAG_Y1 = 3
LAG_Y2 = 5


def choose(j, tiles):
    low = jnp.where(j == 0, tiles[0], tiles[1])
    high = jnp.where(j == 2, tiles[2], tiles[3])
    return jnp.where(j < 2, low, high)


def kernel(integrals, amplitudes, cols_in, out,
           tile_cols, raw0, raw1, ints, a0, a1, a2, a3, a4, a5, a6, a7, keep, give, got, y1, y2, zgot,
           load_t, load_a, load_i, a_send, a_recv, af_send, af_recv,
           i_send, i_recv, if_send, c_send, c_recv,
           y1_send, y1_recv, y2_send, y2_recv, z_send, z_recv):
    x = lax.axis_index("row")
    zl = lax.axis_index("col")
    p = lax.axis_index("rep")
    zh = p // 8
    y = lax.rem(p // 2, 4)
    core = lax.rem(p, 2)
    z = zh * 4 + zl
    xr, xl = lax.rem(x + 1, 4), lax.rem(x + 3, 4)
    yr, yl, yo = lax.rem(y + 1, 4), lax.rem(y + 3, 4), lax.rem(y + 2, 4)

    def at_x(v):
        return (v, zl, p)

    def at_y(v):
        return (x, zl, zh * 8 + v * 2 + core)

    def at_z(v):
        v = lax.rem(v + 8, 8)
        return (x, lax.rem(v, 4), (v // 4) * 8 + y * 2 + core)

    other_core = (x, zl, zh * 8 + y * 2 + (1 - core))

    def remote(src, dst, send, recv, dev):
        return pltpu.make_async_remote_copy(
            src_ref=src, dst_ref=dst, send_sem=send, recv_sem=recv,
            device_id=dev, device_id_type=MESH)

    def half(m):
        return (1 - zh) * (1 - m) + zh * m

    raw = (raw0, raw1)
    amps = (a0, a1, a2, a3, a4, a5, a6, a7)

    def i_load(m):
        rows = pl.ds(pl.multiple_of(half(m) * 1024, 1024), 1024)
        return pltpu.make_async_copy(integrals.at[rows], raw[m], load_i.at[m])

    t_load = pltpu.make_async_copy(cols_in, tile_cols, load_t)
    t_load.start()
    for m in range(2):
        i_load(m).start()

    def a_load(q):
        cols = pl.ds(pl.multiple_of(q * TILE, TILE), TILE)
        return pltpu.make_async_copy(amplitudes.at[:, cols], amps[q].at[x], load_a.at[q])

    for q in range(NQ):
        a_load(q).start()

    barrier = pltpu.get_barrier_semaphore()
    partners = [at_x(xr), at_x(xl), at_y(yr), at_y(yl), at_z(z + 1), at_z(z - 1),
                at_z(z + 2), at_z(z - 2), at_z(z + 4), other_core]
    for dev in partners:
        pl.semaphore_signal(barrier, inc=1, device_id=dev, device_id_type=MESH)

    def pack(m):
        i_load(m).wait()
        group = zl * 16 + p
        for k in range(8):
            i = half(m) * 8 + k
            j = tile_cols[i, group] - group * 4
            rows = pl.ds(k * TILE, TILE)
            ints[zl, i] = choose(j, [raw[m][rows, pl.ds(n * TILE, TILE)] for n in range(4)])

    def i_copy(u, h, send, target):
        part = ints.at[h, pl.ds(half(u // 2) * 8, 8), pl.ds(u % 2 * HALF, HALF)]
        return remote(part, part, send, i_recv.at[u, h], at_z(zh * 4 + target))

    steps = ((0, 2), (1, -2), (2, 1), (3, -1))

    def i_own(u, wait):
        for s, d in steps:
            @pl.when((zl + d >= 0) & (zl + d < 4))
            def _():
                copy = i_copy(u, zl, i_send.at[u, s], zl + d)
                if wait:
                    copy.wait_send()
                else:
                    copy.start()

    def i_forward(u, wait):
        @pl.when((zl == 1) | (zl == 2))
        def _():
            h = jnp.where(zl == 2, 0, 3)
            copy = i_copy(u, h, if_send.at[u], jnp.where(zl == 2, 3, 0))
            if wait:
                copy.wait_send()
            else:
                copy.wait_recv()
                copy.start()

    def i_arrive(u):
        for d in range(1, 4):
            h = lax.rem(zl + d, 4)

            @pl.when(jnp.logical_not(((zl == 2) & (h == 0)) | ((zl == 1) & (h == 3))))
            def _():
                i_copy(u, h, if_send.at[u], zl).wait_recv()

    def a_own(q, d):
        part = amps[q].at[x]
        return remote(part, part, a_send.at[q, d], a_recv.at[q, d], at_x((xr, xl)[d]))

    def a_from(q, d):
        part = amps[q].at[(xl, xr)[d]]
        return remote(part, part, a_send.at[q, d], a_recv.at[q, d], at_x((xr, xl)[d]))

    def a_pass(q, d):
        part = amps[q].at[(xl, xr)[d], pl.ds(d * 256, 256)]
        return remote(part, part, af_send.at[q, d], af_recv.at[q, d], at_x((xr, xl)[d]))

    def a_passed(q, d):
        part = amps[q].at[lax.rem(x + 2, 4), pl.ds(d * 256, 256)]
        return remote(part, part, af_send.at[q, d], af_recv.at[q, d], at_x((xr, xl)[d]))

    def a_start(q):
        a_load(q).wait()
        for d in range(2):
            a_own(q, d).start()

    t_load.wait()
    pack(0)
    pl.semaphore_wait(barrier, len(partners))
    i_own(0, False)
    for q in range(AHEAD):
        a_start(q)
    i_own(1, False)
    pack(1)

    def product(c, u, pair, cc, dst):
        for yy in range(4):
            i = half(u // 2) * 8 + yy * 2 + cc
            rows = pl.ds(pl.multiple_of(lax.rem(u, 2) * HALF, HALF), HALF)
            lhs, rhs = [], []
            for h in range(4):
                group = h * 16 + p
                j = tile_cols[i, group] - group * 4
                lhs.append(ints[h, i, rows])
                rhs.append(jnp.concatenate(
                    [choose(j, [amps[q][h, pl.ds(n * TILE, TILE)] for n in range(4)])
                     for q in (pair * 2, pair * 2 + 1)], axis=1))
            dst[c, yy] = jnp.dot(jnp.concatenate(lhs, axis=1), jnp.concatenate(rhs, axis=0),
                                 preferred_element_type=F32)

    def core_copy(c):
        return remote(give.at[c], got.at[c], c_send, c_recv.at[c], other_core)

    def y1_copy(c, d):
        return remote(keep.at[c, yo, pl.ds(d * 32, 32)], y1.at[c, d], y1_send, y1_recv.at[c, d],
                      at_y((yr, yl)[d]))

    def y2_copy(c, d):
        return remote(keep.at[c, (yr, yl)[d]], y2.at[c, d], y2_send, y2_recv.at[c, d],
                      at_y((yr, yl)[d]))

    def z_copy(c, u, pair):
        return remote(keep.at[c, y], zgot.at[lax.rem(u, 2), pair], z_send,
                      z_recv.at[lax.rem(u, 2), pair], at_z(z + 4))

    def table(t, ticks, values, none):
        found = jnp.int32(none)
        for at, value in zip(ticks, values):
            found = jnp.where(t == at, value, found)
        return found

    def tick(t, carry):
        for q in range(NQ):
            @pl.when(t == A_TICK[q])
            def _():
                for d in range(2):
                    a_from(q, d).wait_recv()
                    a_pass(q, d).start()
                if q + AHEAD < NQ:
                    a_start(q + AHEAD)

        for u in range(4):
            @pl.when(t == I_TICK[u])
            def _():
                i_forward(u, False)
                if u + 2 < 4:
                    i_own(u + 2, False)

        c = table(t, C_TICK, range(NC), -1)
        pair = table(t, C_TICK, [o[1] for o in ORDER], -1)
        u = table(t, C_TICK, [o[0] for o in ORDER], 0)
        for w in range(4):
            @pl.when(t == C_TICK[ORDER.index((w, 0))])
            def _():
                i_arrive(w)

            @pl.when(t == C_TICK[ORDER.index((0, w))])
            def _():
                for q in (w * 2, w * 2 + 1):
                    for d in range(2):
                        a_passed(q, d).wait_recv()

        for w in range(4):
            @pl.when(pair == w)
            def _():
                product(c, u, w, 1 - core, give)
                core_copy(c).start()
                product(c, u, w, core, keep)

        c1 = table(t - LAG_CORE, C_TICK, range(NC), -1)

        @pl.when(c1 >= 0)
        def _():
            core_copy(c1).wait_recv()
            keep[c1, yo] += got[c1, yo]
            for d in range(2):
                y1_copy(c1, d).start()
            for v in (yr, yl, y):
                keep[c1, v] += got[c1, v]

        c2 = table(t - LAG_Y1, C_TICK, range(NC), -1)

        @pl.when(c2 >= 0)
        def _():
            for d in range(2):
                y1_copy(c2, d).wait_recv()
                keep[c2, (yr, yl)[d], pl.ds(d * 32, 32)] += y1[c2, d]
                y2_copy(c2, d).start()

        c3 = table(t - LAG_Y2, C_TICK, range(NC), -1)
        pair3 = table(t - LAG_Y2, C_TICK, [o[1] for o in ORDER], 0)
        u3 = table(t - LAG_Y2, C_TICK, [o[0] for o in ORDER], 0)

        @pl.when(c3 >= 0)
        def _():
            for d in range(2):
                y2_copy(c3, d).wait_recv()

            @pl.when(u3 < 2)
            def _():
                keep[c3, y] += y2[c3, 0] + y2[c3, 1]
                z_copy(c3, u3, pair3).start()

            @pl.when(u3 >= 2)
            def _():
                z_copy(c3, u3, pair3).wait_recv()
                total = (keep[c3, y] + y2[c3, 0]) + (y2[c3, 1] + zgot[u3 - 2, pair3])
                out[pl.ds(pl.multiple_of((u3 - 2) * HALF, HALF), HALF),
                    pl.ds(pl.multiple_of(pair3 * WIDE, WIDE), WIDE)] = total.astype(BF16)

        return carry

    lax.fori_loop(0, C_TICK[-1] + LAG_Y2 + 1, tick, 0)

    for u in range(4):
        i_own(u, True)
        i_forward(u, True)
    for d in range(2):
        for q in range(NQ):
            a_own(q, d).wait_send()
            a_pass(q, d).wait_send()
    for buf, sem in ((give, c_send), (y1, y1_send), (y2, y2_send), (zgot, z_send)):
        remote(buf, buf, sem, c_recv.at[0], other_core).wait_send()


def body(integrals, amplitudes, tile_cols):
    dma = pltpu.SemaphoreType.DMA
    return pl.pallas_call(
        kernel,
        out_shape=jax.ShapeDtypeStruct((TILE, 1024), BF16),
        in_specs=[pl.BlockSpec(memory_space=pltpu.HBM)] * 3,
        out_specs=pl.BlockSpec(memory_space=pltpu.VMEM),
        scratch_shapes=[
            pltpu.SMEM((16, 64), jnp.int32),
            *[pltpu.VMEM((1024, 512), BF16)] * 2,
            pltpu.VMEM((4, 16, TILE, TILE), BF16),
            *[pltpu.VMEM((4, 512, TILE), BF16)] * NQ,
            *[pltpu.VMEM((NC, 4, HALF, WIDE), F32)] * 3,
            pltpu.VMEM((NC, 2, HALF // 2, WIDE), F32),
            pltpu.VMEM((NC, 2, HALF, WIDE), F32),
            pltpu.VMEM((2, 4, HALF, WIDE), F32),
            dma, dma((NQ,)), dma((2,)), *[dma((NQ, 2))] * 4,
            dma((4, 4)), dma((4, 4)), dma((4,)), dma, dma((NC,)),
            dma, dma((NC, 2)), dma, dma((NC, 2)), dma, dma((2, 4)),
        ],
        compiler_params=pltpu.CompilerParams(
            collective_id=0, has_side_effects=True, vmem_limit_bytes=60 << 20),
        cost_estimate=pl.CostEstimate(flops=2 << 30, bytes_accessed=4 << 20, transcendentals=0),
    )(integrals, amplitudes, tile_cols)


def solution(mesh):
    return jax.shard_map(
        body,
        mesh=mesh,
        in_specs=(P("row", ("col", "rep")), P(("row", "rep"), "col"), P("row", None)),
        out_specs=P(("row", "rep"), "col"),
        check_vma=False,
    )
```

```python
import jax
import jax.numpy as jnp
from jax import lax
from jax.experimental import pallas as pl
from jax.experimental.pallas import tpu as pltpu
from jax.sharding import PartitionSpec as P

TILE = 128
MESH = pl.DeviceIdType.MESH
BF16 = jnp.bfloat16
F32 = jnp.float32

NQ = 8
HALF = 64
WIDE = 256
ORDER = ((0, 0), (1, 0), (0, 1), (1, 1), (2, 0), (2, 1), (0, 2), (1, 2),
         (0, 3), (1, 3), (2, 2), (2, 3), (3, 0), (3, 1), (3, 2), (3, 3))
NC = len(ORDER)
A_TICK = (2, 3, 5, 7, 9, 11, 13, 15)
I_TICK = (4, 8, 11, 14)
C_TICK = (8, 10, 12, 13, 14, 15, 16, 17,
         18, 19, 20, 21, 22, 23, 24, 25)
AHEAD = 3
LAG_CORE = 1
LAG_Y1 = 4
LAG_Y2 = 8


def choose(j, tiles):
    low = jnp.where(j == 0, tiles[0], tiles[1])
    high = jnp.where(j == 2, tiles[2], tiles[3])
    return jnp.where(j < 2, low, high)


def kernel(integrals, amplitudes, cols_in, out,
           tile_cols, raw0, raw1, ints, a0, a1, a2, a3, a4, a5, a6, a7, keep, give, got, y1, y2, zgot,
           load_t, load_a, load_i, a_send, a_recv, af_send, af_recv,
           i_send, i_recv, if_send, c_send, c_recv,
           y1_send, y1_recv, y2_send, y2_recv, z_send, z_recv):
    x = lax.axis_index("row")
    zl = lax.axis_index("col")
    p = lax.axis_index("rep")
    zh = p // 8
    y = lax.rem(p // 2, 4)
    core = lax.rem(p, 2)
    z = zh * 4 + zl
    xr, xl = lax.rem(x + 1, 4), lax.rem(x + 3, 4)
    yr, yl, yo = lax.rem(y + 1, 4), lax.rem(y + 3, 4), lax.rem(y + 2, 4)

    def at_x(v):
        return (v, zl, p)

    def at_y(v):
        return (x, zl, zh * 8 + v * 2 + core)

    def at_z(v):
        v = lax.rem(v + 8, 8)
        return (x, lax.rem(v, 4), (v // 4) * 8 + y * 2 + core)

    other_core = (x, zl, zh * 8 + y * 2 + (1 - core))

    def remote(src, dst, send, recv, dev):
        return pltpu.make_async_remote_copy(
            src_ref=src, dst_ref=dst, send_sem=send, recv_sem=recv,
            device_id=dev, device_id_type=MESH)

    def half(m):
        return (1 - zh) * (1 - m) + zh * m

    raw = (raw0, raw1)
    amps = (a0, a1, a2, a3, a4, a5, a6, a7)

    def i_load(m):
        rows = pl.ds(pl.multiple_of(half(m) * 1024, 1024), 1024)
        return pltpu.make_async_copy(integrals.at[rows], raw[m], load_i.at[m])

    t_load = pltpu.make_async_copy(cols_in, tile_cols, load_t)
    t_load.start()
    for m in range(2):
        i_load(m).start()

    def a_load(q):
        cols = pl.ds(pl.multiple_of(q * TILE, TILE), TILE)
        return pltpu.make_async_copy(amplitudes.at[:, cols], amps[q].at[x], load_a.at[q])

    for q in range(NQ):
        a_load(q).start()

    barrier = pltpu.get_barrier_semaphore()
    partners = [at_x(xr), at_x(xl), at_y(yr), at_y(yl), at_z(z + 1), at_z(z - 1),
                at_z(z + 2), at_z(z - 2), at_z(z + 4), other_core]
    for dev in partners:
        pl.semaphore_signal(barrier, inc=1, device_id=dev, device_id_type=MESH)

    def pack(m):
        i_load(m).wait()
        group = zl * 16 + p
        for k in range(8):
            i = half(m) * 8 + k
            j = tile_cols[i, group] - group * 4
            rows = pl.ds(k * TILE, TILE)
            ints[zl, i] = choose(j, [raw[m][rows, pl.ds(n * TILE, TILE)] for n in range(4)])

    def i_copy(u, h, send, target):
        part = ints.at[h, pl.ds(half(u // 2) * 8, 8), pl.ds(u % 2 * HALF, HALF)]
        return remote(part, part, send, i_recv.at[u, h], at_z(zh * 4 + target))

    steps = ((0, 2), (1, -2), (2, 1), (3, -1))

    def i_own(u, wait):
        for s, d in steps:
            @pl.when((zl + d >= 0) & (zl + d < 4))
            def _():
                copy = i_copy(u, zl, i_send.at[u, s], zl + d)
                if wait:
                    copy.wait_send()
                else:
                    copy.start()

    def i_forward(u, wait):
        @pl.when((zl == 1) | (zl == 2))
        def _():
            h = jnp.where(zl == 2, 0, 3)
            copy = i_copy(u, h, if_send.at[u], jnp.where(zl == 2, 3, 0))
            if wait:
                copy.wait_send()
            else:
                copy.wait_recv()
                copy.start()

    def i_arrive(u):
        for d in range(1, 4):
            h = lax.rem(zl + d, 4)

            @pl.when(jnp.logical_not(((zl == 2) & (h == 0)) | ((zl == 1) & (h == 3))))
            def _():
                i_copy(u, h, if_send.at[u], zl).wait_recv()

    def a_own(q, d):
        part = amps[q].at[x]
        return remote(part, part, a_send.at[q, d], a_recv.at[q, d], at_x((xr, xl)[d]))

    def a_from(q, d):
        part = amps[q].at[(xl, xr)[d]]
        return remote(part, part, a_send.at[q, d], a_recv.at[q, d], at_x((xr, xl)[d]))

    def a_pass(q, d):
        part = amps[q].at[(xl, xr)[d], pl.ds(d * 256, 256)]
        return remote(part, part, af_send.at[q, d], af_recv.at[q, d], at_x((xr, xl)[d]))

    def a_passed(q, d):
        part = amps[q].at[lax.rem(x + 2, 4), pl.ds(d * 256, 256)]
        return remote(part, part, af_send.at[q, d], af_recv.at[q, d], at_x((xr, xl)[d]))

    def a_start(q):
        a_load(q).wait()
        for d in range(2):
            a_own(q, d).start()

    t_load.wait()
    pack(0)
    pl.semaphore_wait(barrier, len(partners))
    i_own(0, False)
    for q in range(AHEAD):
        a_start(q)
    i_own(1, False)
    pack(1)

    def product(c, u, pair, cc, dst):
        for yy in range(4):
            i = half(u // 2) * 8 + yy * 2 + cc
            rows = pl.ds(pl.multiple_of(lax.rem(u, 2) * HALF, HALF), HALF)
            lhs, rhs = [], []
            for h in range(4):
                group = h * 16 + p
                j = tile_cols[i, group] - group * 4
                lhs.append(ints[h, i, rows])
                rhs.append(jnp.concatenate(
                    [choose(j, [amps[q][h, pl.ds(n * TILE, TILE)] for n in range(4)])
                     for q in (pair * 2, pair * 2 + 1)], axis=1))
            dst[c, yy] = jnp.dot(jnp.concatenate(lhs, axis=1), jnp.concatenate(rhs, axis=0),
                                 preferred_element_type=F32)

    def core_copy(c):
        return remote(give.at[c], got.at[c], c_send, c_recv.at[c], other_core)

    def y1_copy(c, d):
        return remote(keep.at[c, yo, pl.ds(d * 32, 32)], y1.at[c, d], y1_send, y1_recv.at[c, d],
                      at_y((yr, yl)[d]))

    def y2_copy(c, d):
        return remote(keep.at[c, (yr, yl)[d]], y2.at[c, d], y2_send, y2_recv.at[c, d],
                      at_y((yr, yl)[d]))

    def z_copy(c, u, pair):
        return remote(keep.at[c, y], zgot.at[lax.rem(u, 2), pair], z_send,
                      z_recv.at[lax.rem(u, 2), pair], at_z(z + 4))

    def table(t, ticks, values, none):
        found = jnp.int32(none)
        for at, value in zip(ticks, values):
            found = jnp.where(t == at, value, found)
        return found

    def tick(t, carry):
        for q in range(NQ):
            @pl.when(t == A_TICK[q])
            def _():
                for d in range(2):
                    a_from(q, d).wait_recv()
                    a_pass(q, d).start()
                if q + AHEAD < NQ:
                    a_start(q + AHEAD)

        for u in range(4):
            @pl.when(t == I_TICK[u])
            def _():
                i_forward(u, False)
                if u + 2 < 4:
                    i_own(u + 2, False)

        c = table(t, C_TICK, range(NC), -1)
        pair = table(t, C_TICK, [o[1] for o in ORDER], -1)
        u = table(t, C_TICK, [o[0] for o in ORDER], 0)
        for w in range(4):
            @pl.when(t == C_TICK[min(i for i, o in enumerate(ORDER) if o[0] == w)])
            def _():
                i_arrive(w)

            @pl.when(t == C_TICK[min(i for i, o in enumerate(ORDER) if o[1] == w)])
            def _():
                for q in (w * 2, w * 2 + 1):
                    for d in range(2):
                        a_passed(q, d).wait_recv()

        for w in range(4):
            @pl.when(pair == w)
            def _():
                product(c, u, w, 1 - core, give)
                core_copy(c).start()
                product(c, u, w, core, keep)

        c1 = table(t - LAG_CORE, C_TICK, range(NC), -1)

        @pl.when(c1 >= 0)
        def _():
            core_copy(c1).wait_recv()
            keep[c1, yo] += got[c1, yo]
            for d in range(2):
                y1_copy(c1, d).start()
            for v in (yr, yl, y):
                keep[c1, v] += got[c1, v]

        c2 = table(t - LAG_Y1, C_TICK, range(NC), -1)

        @pl.when(c2 >= 0)
        def _():
            for d in range(2):
                y1_copy(c2, d).wait_recv()
                keep[c2, (yr, yl)[d], pl.ds(d * 32, 32)] += y1[c2, d]
                y2_copy(c2, d).start()

        c3 = table(t - LAG_Y2, C_TICK, range(NC), -1)
        pair3 = table(t - LAG_Y2, C_TICK, [o[1] for o in ORDER], 0)
        u3 = table(t - LAG_Y2, C_TICK, [o[0] for o in ORDER], 0)

        @pl.when(c3 >= 0)
        def _():
            for d in range(2):
                y2_copy(c3, d).wait_recv()

            @pl.when(u3 < 2)
            def _():
                keep[c3, y] += y2[c3, 0] + y2[c3, 1]
                z_copy(c3, u3, pair3).start()

            @pl.when(u3 >= 2)
            def _():
                z_copy(c3, u3, pair3).wait_recv()
                total = (keep[c3, y] + y2[c3, 0]) + (y2[c3, 1] + zgot[u3 - 2, pair3])
                out[pl.ds(pl.multiple_of((u3 - 2) * HALF, HALF), HALF),
                    pl.ds(pl.multiple_of(pair3 * WIDE, WIDE), WIDE)] = total.astype(BF16)

        return carry

    lax.fori_loop(0, C_TICK[-1] + LAG_Y2 + 1, tick, 0)

    for u in range(4):
        i_own(u, True)
        i_forward(u, True)
    for d in range(2):
        for q in range(NQ):
            a_own(q, d).wait_send()
            a_pass(q, d).wait_send()
    for buf, sem in ((give, c_send), (y1, y1_send), (y2, y2_send), (zgot, z_send)):
        remote(buf, buf, sem, c_recv.at[0], other_core).wait_send()


def body(integrals, amplitudes, tile_cols):
    dma = pltpu.SemaphoreType.DMA
    return pl.pallas_call(
        kernel,
        out_shape=jax.ShapeDtypeStruct((TILE, 1024), BF16),
        in_specs=[pl.BlockSpec(memory_space=pltpu.HBM)] * 3,
        out_specs=pl.BlockSpec(memory_space=pltpu.VMEM),
        scratch_shapes=[
            pltpu.SMEM((16, 64), jnp.int32),
            *[pltpu.VMEM((1024, 512), BF16)] * 2,
            pltpu.VMEM((4, 16, TILE, TILE), BF16),
            *[pltpu.VMEM((4, 512, TILE), BF16)] * NQ,
            *[pltpu.VMEM((NC, 4, HALF, WIDE), F32)] * 3,
            pltpu.VMEM((NC, 2, HALF // 2, WIDE), F32),
            pltpu.VMEM((NC, 2, HALF, WIDE), F32),
            pltpu.VMEM((2, 4, HALF, WIDE), F32),
            dma, dma((NQ,)), dma((2,)), *[dma((NQ, 2))] * 4,
            dma((4, 4)), dma((4, 4)), dma((4,)), dma, dma((NC,)),
            dma, dma((NC, 2)), dma, dma((NC, 2)), dma, dma((2, 4)),
        ],
        compiler_params=pltpu.CompilerParams(
            collective_id=0, has_side_effects=True, vmem_limit_bytes=60 << 20),
        cost_estimate=pl.CostEstimate(flops=2 << 30, bytes_accessed=4 << 20, transcendentals=0),
    )(integrals, amplitudes, tile_cols)


def solution(mesh):
    return jax.shard_map(
        body,
        mesh=mesh,
        in_specs=(P("row", ("col", "rep")), P(("row", "rep"), "col"), P("row", None)),
        out_specs=P(("row", "rep"), "col"),
        check_vma=False,
    )
```

```python
import jax
import jax.numpy as jnp
from jax import lax
from jax.experimental import pallas as pl
from jax.experimental.pallas import tpu as pltpu
from jax.sharding import PartitionSpec as P

TILE = 128
MESH = pl.DeviceIdType.MESH
BF16 = jnp.bfloat16
F32 = jnp.float32

NQ = 8
HALF = 64
WIDE = 256
ORDER = ((0, 0), (1, 0), (0, 1), (1, 1), (2, 0), (2, 1), (0, 2), (1, 2),
         (0, 3), (1, 3), (2, 2), (2, 3), (3, 0), (3, 1), (3, 2), (3, 3))
NC = len(ORDER)
A_TICK = (2, 3, 5, 7, 9, 11, 13, 15)
I_TICK = (4, 8, 11, 14)
C_TICK = (8, 10, 12, 13, 14, 15, 16, 17,
         18, 19, 20, 21, 22, 23, 24, 25)
AHEAD = 3
LAG_CORE = 1
LAG_Y1 = 4
LAG_Y2 = 8


def choose(j, tiles):
    low = jnp.where(j == 0, tiles[0], tiles[1])
    high = jnp.where(j == 2, tiles[2], tiles[3])
    return jnp.where(j < 2, low, high)


def kernel(integrals, amplitudes, cols_in, out,
           tile_cols, raw0, raw1, ints, a0, a1, a2, a3, a4, a5, a6, a7, keep, give, got, y1, y2, zgot,
           load_t, load_a, load_i, a_send, a_recv, af_send, af_recv,
           i_send, i_recv, if_send, c_send, c_recv,
           y1_send, y1_recv, y2_send, y2_recv, z_send, z_recv):
    x = lax.axis_index("row")
    zl = lax.axis_index("col")
    p = lax.axis_index("rep")
    zh = p // 8
    y = lax.rem(p // 2, 4)
    core = lax.rem(p, 2)
    z = zh * 4 + zl
    xr, xl = lax.rem(x + 1, 4), lax.rem(x + 3, 4)
    yr, yl, yo = lax.rem(y + 1, 4), lax.rem(y + 3, 4), lax.rem(y + 2, 4)

    def at_x(v):
        return (v, zl, p)

    def at_y(v):
        return (x, zl, zh * 8 + v * 2 + core)

    def at_z(v):
        v = lax.rem(v + 8, 8)
        return (x, lax.rem(v, 4), (v // 4) * 8 + y * 2 + core)

    other_core = (x, zl, zh * 8 + y * 2 + (1 - core))

    def remote(src, dst, send, recv, dev):
        return pltpu.make_async_remote_copy(
            src_ref=src, dst_ref=dst, send_sem=send, recv_sem=recv,
            device_id=dev, device_id_type=MESH)

    def half(m):
        return (1 - zh) * (1 - m) + zh * m

    raw = (raw0, raw1)
    amps = (a0, a1, a2, a3, a4, a5, a6, a7)

    def i_load(m):
        rows = pl.ds(pl.multiple_of(half(m) * 1024, 1024), 1024)
        return pltpu.make_async_copy(integrals.at[rows], raw[m], load_i.at[m])

    t_load = pltpu.make_async_copy(cols_in, tile_cols, load_t)
    t_load.start()
    for m in range(2):
        i_load(m).start()

    def a_load(q):
        cols = pl.ds(pl.multiple_of(q * TILE, TILE), TILE)
        return pltpu.make_async_copy(amplitudes.at[:, cols], amps[q].at[x], load_a.at[q])

    for q in range(NQ):
        a_load(q).start()

    barrier = pltpu.get_barrier_semaphore()
    partners = [at_x(xr), at_x(xl), at_y(yr), at_y(yl), at_z(z + 1), at_z(z - 1),
                at_z(z + 2), at_z(z - 2), at_z(z + 4), other_core]
    for dev in partners:
        pl.semaphore_signal(barrier, inc=1, device_id=dev, device_id_type=MESH)

    def pack(m):
        i_load(m).wait()
        group = zl * 16 + p
        for k in range(8):
            i = half(m) * 8 + k
            j = tile_cols[i, group] - group * 4
            rows = pl.ds(k * TILE, TILE)
            ints[zl, i] = choose(j, [raw[m][rows, pl.ds(n * TILE, TILE)] for n in range(4)])

    def i_copy(u, h, send, target):
        part = ints.at[h, pl.ds(half(u // 2) * 8, 8), pl.ds(u % 2 * HALF, HALF)]
        return remote(part, part, send, i_recv.at[u, h], at_z(zh * 4 + target))

    steps = ((0, 2), (1, -2), (2, 1), (3, -1))

    def i_own(u, wait):
        for s, d in steps:
            @pl.when((zl + d >= 0) & (zl + d < 4))
            def _():
                copy = i_copy(u, zl, i_send.at[u, s], zl + d)
                if wait:
                    copy.wait_send()
                else:
                    copy.start()

    def i_forward(u, wait):
        @pl.when((zl == 1) | (zl == 2))
        def _():
            h = jnp.where(zl == 2, 0, 3)
            copy = i_copy(u, h, if_send.at[u], jnp.where(zl == 2, 3, 0))
            if wait:
                copy.wait_send()
            else:
                copy.wait_recv()
                copy.start()

    def i_arrive(u):
        for d in range(1, 4):
            h = lax.rem(zl + d, 4)

            @pl.when(jnp.logical_not(((zl == 2) & (h == 0)) | ((zl == 1) & (h == 3))))
            def _():
                i_copy(u, h, if_send.at[u], zl).wait_recv()

    def a_own(q, d):
        part = amps[q].at[x]
        return remote(part, part, a_send.at[q, d], a_recv.at[q, d], at_x((xr, xl)[d]))

    def a_from(q, d):
        part = amps[q].at[(xl, xr)[d]]
        return remote(part, part, a_send.at[q, d], a_recv.at[q, d], at_x((xr, xl)[d]))

    def a_pass(q, d):
        part = amps[q].at[(xl, xr)[d], pl.ds(d * 256, 256)]
        return remote(part, part, af_send.at[q, d], af_recv.at[q, d], at_x((xr, xl)[d]))

    def a_passed(q, d):
        part = amps[q].at[lax.rem(x + 2, 4), pl.ds(d * 256, 256)]
        return remote(part, part, af_send.at[q, d], af_recv.at[q, d], at_x((xr, xl)[d]))

    def a_start(q):
        a_load(q).wait()
        for d in range(2):
            a_own(q, d).start()

    pl.semaphore_wait(barrier, len(partners))
    a_start(0)
    t_load.wait()
    pack(0)
    i_own(0, False)
    for q in range(1, AHEAD):
        a_start(q)
    i_own(1, False)
    pack(1)

    def product(c, u, pair, cc, dst):
        for yy in range(4):
            i = half(u // 2) * 8 + yy * 2 + cc
            rows = pl.ds(pl.multiple_of(lax.rem(u, 2) * HALF, HALF), HALF)
            lhs, rhs = [], []
            for h in range(4):
                group = h * 16 + p
                j = tile_cols[i, group] - group * 4
                lhs.append(ints[h, i, rows])
                rhs.append(jnp.concatenate(
                    [choose(j, [amps[q][h, pl.ds(n * TILE, TILE)] for n in range(4)])
                     for q in (pair * 2, pair * 2 + 1)], axis=1))
            dst[c, yy] = jnp.dot(jnp.concatenate(lhs, axis=1), jnp.concatenate(rhs, axis=0),
                                 preferred_element_type=F32)

    def core_copy(c):
        return remote(give.at[c], got.at[c], c_send, c_recv.at[c], other_core)

    def y1_copy(c, d):
        return remote(keep.at[c, yo, pl.ds(d * 32, 32)], y1.at[c, d], y1_send, y1_recv.at[c, d],
                      at_y((yr, yl)[d]))

    def y2_copy(c, d):
        return remote(keep.at[c, (yr, yl)[d]], y2.at[c, d], y2_send, y2_recv.at[c, d],
                      at_y((yr, yl)[d]))

    def z_copy(c, u, pair):
        return remote(keep.at[c, y], zgot.at[lax.rem(u, 2), pair], z_send,
                      z_recv.at[lax.rem(u, 2), pair], at_z(z + 4))

    def table(t, ticks, values, none):
        found = jnp.int32(none)
        for at, value in zip(ticks, values):
            found = jnp.where(t == at, value, found)
        return found

    def tick(t, carry):
        for q in range(NQ):
            @pl.when(t == A_TICK[q])
            def _():
                for d in range(2):
                    a_from(q, d).wait_recv()
                    a_pass(q, d).start()
                if q + AHEAD < NQ:
                    a_start(q + AHEAD)

        for u in range(4):
            @pl.when(t == I_TICK[u])
            def _():
                i_forward(u, False)
                if u + 2 < 4:
                    i_own(u + 2, False)

        c = table(t, C_TICK, range(NC), -1)
        pair = table(t, C_TICK, [o[1] for o in ORDER], -1)
        u = table(t, C_TICK, [o[0] for o in ORDER], 0)
        for w in range(4):
            @pl.when(t == C_TICK[min(i for i, o in enumerate(ORDER) if o[0] == w)])
            def _():
                i_arrive(w)

            @pl.when(t == C_TICK[min(i for i, o in enumerate(ORDER) if o[1] == w)])
            def _():
                for q in (w * 2, w * 2 + 1):
                    for d in range(2):
                        a_passed(q, d).wait_recv()

        for w in range(4):
            @pl.when(pair == w)
            def _():
                product(c, u, w, 1 - core, give)
                core_copy(c).start()
                product(c, u, w, core, keep)

        c1 = table(t - LAG_CORE, C_TICK, range(NC), -1)

        @pl.when(c1 >= 0)
        def _():
            core_copy(c1).wait_recv()
            keep[c1, yo] += got[c1, yo]
            for d in range(2):
                y1_copy(c1, d).start()
            for v in (yr, yl, y):
                keep[c1, v] += got[c1, v]

        c2 = table(t - LAG_Y1, C_TICK, range(NC), -1)

        @pl.when(c2 >= 0)
        def _():
            for d in range(2):
                y1_copy(c2, d).wait_recv()
                keep[c2, (yr, yl)[d], pl.ds(d * 32, 32)] += y1[c2, d]
                y2_copy(c2, d).start()

        c3 = table(t - LAG_Y2, C_TICK, range(NC), -1)
        pair3 = table(t - LAG_Y2, C_TICK, [o[1] for o in ORDER], 0)
        u3 = table(t - LAG_Y2, C_TICK, [o[0] for o in ORDER], 0)

        @pl.when(c3 >= 0)
        def _():
            for d in range(2):
                y2_copy(c3, d).wait_recv()

            @pl.when(u3 < 2)
            def _():
                keep[c3, y] += y2[c3, 0] + y2[c3, 1]
                z_copy(c3, u3, pair3).start()

            @pl.when(u3 >= 2)
            def _():
                z_copy(c3, u3, pair3).wait_recv()
                total = (keep[c3, y] + y2[c3, 0]) + (y2[c3, 1] + zgot[u3 - 2, pair3])
                out[pl.ds(pl.multiple_of((u3 - 2) * HALF, HALF), HALF),
                    pl.ds(pl.multiple_of(pair3 * WIDE, WIDE), WIDE)] = total.astype(BF16)

        return carry

    lax.fori_loop(0, C_TICK[-1] + LAG_Y2 + 1, tick, 0)

    for u in range(4):
        i_own(u, True)
        i_forward(u, True)
    for d in range(2):
        for q in range(NQ):
            a_own(q, d).wait_send()
            a_pass(q, d).wait_send()
    for buf, sem in ((give, c_send), (y1, y1_send), (y2, y2_send), (zgot, z_send)):
        remote(buf, buf, sem, c_recv.at[0], other_core).wait_send()


def body(integrals, amplitudes, tile_cols):
    dma = pltpu.SemaphoreType.DMA
    return pl.pallas_call(
        kernel,
        out_shape=jax.ShapeDtypeStruct((TILE, 1024), BF16),
        in_specs=[pl.BlockSpec(memory_space=pltpu.HBM)] * 3,
        out_specs=pl.BlockSpec(memory_space=pltpu.VMEM),
        scratch_shapes=[
            pltpu.SMEM((16, 64), jnp.int32),
            *[pltpu.VMEM((1024, 512), BF16)] * 2,
            pltpu.VMEM((4, 16, TILE, TILE), BF16),
            *[pltpu.VMEM((4, 512, TILE), BF16)] * NQ,
            *[pltpu.VMEM((NC, 4, HALF, WIDE), F32)] * 3,
            pltpu.VMEM((NC, 2, HALF // 2, WIDE), F32),
            pltpu.VMEM((NC, 2, HALF, WIDE), F32),
            pltpu.VMEM((2, 4, HALF, WIDE), F32),
            dma, dma((NQ,)), dma((2,)), *[dma((NQ, 2))] * 4,
            dma((4, 4)), dma((4, 4)), dma((4,)), dma, dma((NC,)),
            dma, dma((NC, 2)), dma, dma((NC, 2)), dma, dma((2, 4)),
        ],
        compiler_params=pltpu.CompilerParams(
            collective_id=0, has_side_effects=True, vmem_limit_bytes=53 << 20),
        cost_estimate=pl.CostEstimate(flops=2 << 30, bytes_accessed=4 << 20, transcendentals=0),
    )(integrals, amplitudes, tile_cols)


def solution(mesh):
    return jax.shard_map(
        body,
        mesh=mesh,
        in_specs=(P("row", ("col", "rep")), P(("row", "rep"), "col"), P("row", None)),
        out_specs=P(("row", "rep"), "col"),
        check_vma=False,
    )
```

```python
import jax
import jax.numpy as jnp
from jax import lax
from jax.experimental import pallas as pl
from jax.experimental.pallas import tpu as pltpu
from jax.sharding import PartitionSpec as P

TILE = 128
MESH = pl.DeviceIdType.MESH
BF16 = jnp.bfloat16
F32 = jnp.float32

NQ = 8
HALF = 64
WIDE = 256
ORDER = ((0, 0), (1, 0), (0, 1), (1, 1), (2, 0), (2, 1), (0, 2), (1, 2),
         (0, 3), (1, 3), (2, 2), (2, 3), (3, 0), (3, 1), (3, 2), (3, 3))
NC = len(ORDER)
A_TICK = (2, 3, 5, 7, 9, 11, 14, 18)
I_TICK = (4, 8, 11, 15)
C_TICK = (8, 10, 12, 13, 16, 17, 19, 20, 21, 22, 23, 24, 25, 26, 27, 28)
AHEAD = 3
LAG_CORE = 1
LAG_Y1 = 4
LAG_Y2 = 8


def choose(j, tiles):
    low = jnp.where(j == 0, tiles[0], tiles[1])
    high = jnp.where(j == 2, tiles[2], tiles[3])
    return jnp.where(j < 2, low, high)


def kernel(integrals, amplitudes, cols_in, out,
           tile_cols, raw0, raw1, ints, a0, a1, a2, a3, a4, a5, a6, a7, keep, give, got, y1, y2, zgot,
           load_t, load_a, load_i, a_send, a_recv, af_send, af_recv,
           i_send, i_recv, if_send, c_send, c_recv,
           y1_send, y1_recv, y2_send, y2_recv, z_send, z_recv):
    x = lax.axis_index("row")
    zl = lax.axis_index("col")
    p = lax.axis_index("rep")
    zh = p // 8
    y = lax.rem(p // 2, 4)
    core = lax.rem(p, 2)
    z = zh * 4 + zl
    xr, xl = lax.rem(x + 1, 4), lax.rem(x + 3, 4)
    yr, yl, yo = lax.rem(y + 1, 4), lax.rem(y + 3, 4), lax.rem(y + 2, 4)

    def at_x(v):
        return (v, zl, p)

    def at_y(v):
        return (x, zl, zh * 8 + v * 2 + core)

    def at_z(v):
        v = lax.rem(v + 8, 8)
        return (x, lax.rem(v, 4), (v // 4) * 8 + y * 2 + core)

    other_core = (x, zl, zh * 8 + y * 2 + (1 - core))

    def remote(src, dst, send, recv, dev):
        return pltpu.make_async_remote_copy(
            src_ref=src, dst_ref=dst, send_sem=send, recv_sem=recv,
            device_id=dev, device_id_type=MESH)

    def half(m):
        return (1 - zh) * (1 - m) + zh * m

    raw = (raw0, raw1)
    amps = (a0, a1, a2, a3, a4, a5, a6, a7)

    def i_load(m):
        rows = pl.ds(pl.multiple_of(half(m) * 1024, 1024), 1024)
        return pltpu.make_async_copy(integrals.at[rows], raw[m], load_i.at[m])

    t_load = pltpu.make_async_copy(cols_in, tile_cols, load_t)
    t_load.start()
    for m in range(2):
        i_load(m).start()

    def a_load(q):
        cols = pl.ds(pl.multiple_of(q * TILE, TILE), TILE)
        return pltpu.make_async_copy(amplitudes.at[:, cols], amps[q].at[x], load_a.at[q])

    for q in range(NQ):
        a_load(q).start()

    barrier = pltpu.get_barrier_semaphore()
    partners = [at_x(xr), at_x(xl), at_y(yr), at_y(yl), at_z(z + 1), at_z(z - 1),
                at_z(z + 2), at_z(z - 2), at_z(z + 4), other_core]
    for dev in partners:
        pl.semaphore_signal(barrier, inc=1, device_id=dev, device_id_type=MESH)

    def pack(m):
        i_load(m).wait()
        group = zl * 16 + p
        for k in range(8):
            i = half(m) * 8 + k
            j = tile_cols[i, group] - group * 4
            rows = pl.ds(k * TILE, TILE)
            ints[zl, i] = choose(j, [raw[m][rows, pl.ds(n * TILE, TILE)] for n in range(4)])

    def i_copy(u, h, send, target):
        part = ints.at[h, pl.ds(half(u // 2) * 8, 8), pl.ds(u % 2 * HALF, HALF)]
        return remote(part, part, send, i_recv.at[u, h], at_z(zh * 4 + target))

    steps = ((0, 2), (1, -2), (2, 1), (3, -1))

    def i_own(u, wait):
        for s, d in steps:
            @pl.when((zl + d >= 0) & (zl + d < 4))
            def _():
                copy = i_copy(u, zl, i_send.at[u, s], zl + d)
                if wait:
                    copy.wait_send()
                else:
                    copy.start()

    def i_forward(u, wait):
        @pl.when((zl == 1) | (zl == 2))
        def _():
            h = jnp.where(zl == 2, 0, 3)
            copy = i_copy(u, h, if_send.at[u], jnp.where(zl == 2, 3, 0))
            if wait:
                copy.wait_send()
            else:
                copy.wait_recv()
                copy.start()

    def i_arrive(u):
        for d in range(1, 4):
            h = lax.rem(zl + d, 4)

            @pl.when(jnp.logical_not(((zl == 2) & (h == 0)) | ((zl == 1) & (h == 3))))
            def _():
                i_copy(u, h, if_send.at[u], zl).wait_recv()

    def a_own(q, d):
        part = amps[q].at[x]
        return remote(part, part, a_send.at[q, d], a_recv.at[q, d], at_x((xr, xl)[d]))

    def a_from(q, d):
        part = amps[q].at[(xl, xr)[d]]
        return remote(part, part, a_send.at[q, d], a_recv.at[q, d], at_x((xr, xl)[d]))

    def a_pass(q, d):
        part = amps[q].at[(xl, xr)[d], pl.ds(d * 256, 256)]
        return remote(part, part, af_send.at[q, d], af_recv.at[q, d], at_x((xr, xl)[d]))

    def a_passed(q, d):
        part = amps[q].at[lax.rem(x + 2, 4), pl.ds(d * 256, 256)]
        return remote(part, part, af_send.at[q, d], af_recv.at[q, d], at_x((xr, xl)[d]))

    def a_start(q):
        a_load(q).wait()
        for d in range(2):
            a_own(q, d).start()

    pl.semaphore_wait(barrier, len(partners))
    a_start(0)
    t_load.wait()
    pack(0)
    i_own(0, False)
    for q in range(1, AHEAD):
        a_start(q)
    i_own(1, False)
    pack(1)

    def product(c, u, pair, cc, dst):
        for yy in range(4):
            i = half(u // 2) * 8 + yy * 2 + cc
            rows = pl.ds(pl.multiple_of(lax.rem(u, 2) * HALF, HALF), HALF)
            lhs, rhs = [], []
            for h in range(4):
                group = h * 16 + p
                j = tile_cols[i, group] - group * 4
                lhs.append(ints[h, i, rows])
                rhs.append(jnp.concatenate(
                    [choose(j, [amps[q][h, pl.ds(n * TILE, TILE)] for n in range(4)])
                     for q in (pair * 2, pair * 2 + 1)], axis=1))
            dst[c, yy] = jnp.dot(jnp.concatenate(lhs, axis=1), jnp.concatenate(rhs, axis=0),
                                 preferred_element_type=F32)

    def core_copy(c):
        return remote(give.at[c], got.at[c], c_send, c_recv.at[c], other_core)

    def y1_copy(c, d):
        return remote(keep.at[c, yo, pl.ds(d * 32, 32)], y1.at[c, d], y1_send, y1_recv.at[c, d],
                      at_y((yr, yl)[d]))

    def y2_copy(c, d):
        return remote(keep.at[c, (yr, yl)[d]], y2.at[c, d], y2_send, y2_recv.at[c, d],
                      at_y((yr, yl)[d]))

    def z_copy(c, u, pair):
        return remote(keep.at[c, y], zgot.at[lax.rem(u, 2), pair], z_send,
                      z_recv.at[lax.rem(u, 2), pair], at_z(z + 4))

    def table(t, ticks, values, none):
        found = jnp.int32(none)
        for at, value in zip(ticks, values):
            found = jnp.where(t == at, value, found)
        return found

    def tick(t, carry):
        for q in range(NQ):
            @pl.when(t == A_TICK[q])
            def _():
                for d in range(2):
                    a_from(q, d).wait_recv()
                    a_pass(q, d).start()
                if q + AHEAD < NQ:
                    a_start(q + AHEAD)

        for u in range(4):
            @pl.when(t == I_TICK[u])
            def _():
                i_forward(u, False)
                if u + 2 < 4:
                    i_own(u + 2, False)

        c = table(t, C_TICK, range(NC), -1)
        pair = table(t, C_TICK, [o[1] for o in ORDER], -1)
        u = table(t, C_TICK, [o[0] for o in ORDER], 0)
        for w in range(4):
            @pl.when(t == C_TICK[min(i for i, o in enumerate(ORDER) if o[0] == w)])
            def _():
                i_arrive(w)

            @pl.when(t == C_TICK[min(i for i, o in enumerate(ORDER) if o[1] == w)])
            def _():
                for q in (w * 2, w * 2 + 1):
                    for d in range(2):
                        a_passed(q, d).wait_recv()

        for w in range(4):
            @pl.when(pair == w)
            def _():
                product(c, u, w, 1 - core, give)
                core_copy(c).start()
                product(c, u, w, core, keep)

        c1 = table(t - LAG_CORE, C_TICK, range(NC), -1)

        @pl.when(c1 >= 0)
        def _():
            core_copy(c1).wait_recv()
            keep[c1, yo] += got[c1, yo]
            for d in range(2):
                y1_copy(c1, d).start()
            for v in (yr, yl, y):
                keep[c1, v] += got[c1, v]

        c2 = table(t - LAG_Y1, C_TICK, range(NC), -1)

        @pl.when(c2 >= 0)
        def _():
            for d in range(2):
                y1_copy(c2, d).wait_recv()
                keep[c2, (yr, yl)[d], pl.ds(d * 32, 32)] += y1[c2, d]
                y2_copy(c2, d).start()

        c3 = table(t - LAG_Y2, C_TICK, range(NC), -1)
        pair3 = table(t - LAG_Y2, C_TICK, [o[1] for o in ORDER], 0)
        u3 = table(t - LAG_Y2, C_TICK, [o[0] for o in ORDER], 0)

        @pl.when(c3 >= 0)
        def _():
            for d in range(2):
                y2_copy(c3, d).wait_recv()

            @pl.when(u3 < 2)
            def _():
                keep[c3, y] += y2[c3, 0] + y2[c3, 1]
                z_copy(c3, u3, pair3).start()

            @pl.when(u3 >= 2)
            def _():
                z_copy(c3, u3, pair3).wait_recv()
                total = (keep[c3, y] + y2[c3, 0]) + (y2[c3, 1] + zgot[u3 - 2, pair3])
                out[pl.ds(pl.multiple_of((u3 - 2) * HALF, HALF), HALF),
                    pl.ds(pl.multiple_of(pair3 * WIDE, WIDE), WIDE)] = total.astype(BF16)

        return carry

    lax.fori_loop(0, C_TICK[-1] + LAG_Y2 + 1, tick, 0)

    for u in range(4):
        i_own(u, True)
        i_forward(u, True)
    for d in range(2):
        for q in range(NQ):
            a_own(q, d).wait_send()
            a_pass(q, d).wait_send()
    for buf, sem in ((give, c_send), (y1, y1_send), (y2, y2_send), (zgot, z_send)):
        remote(buf, buf, sem, c_recv.at[0], other_core).wait_send()


def body(integrals, amplitudes, tile_cols):
    dma = pltpu.SemaphoreType.DMA
    return pl.pallas_call(
        kernel,
        out_shape=jax.ShapeDtypeStruct((TILE, 1024), BF16),
        in_specs=[pl.BlockSpec(memory_space=pltpu.HBM)] * 3,
        out_specs=pl.BlockSpec(memory_space=pltpu.VMEM),
        scratch_shapes=[
            pltpu.SMEM((16, 64), jnp.int32),
            *[pltpu.VMEM((1024, 512), BF16)] * 2,
            pltpu.VMEM((4, 16, TILE, TILE), BF16),
            *[pltpu.VMEM((4, 512, TILE), BF16)] * NQ,
            *[pltpu.VMEM((NC, 4, HALF, WIDE), F32)] * 3,
            pltpu.VMEM((NC, 2, HALF // 2, WIDE), F32),
            pltpu.VMEM((NC, 2, HALF, WIDE), F32),
            pltpu.VMEM((2, 4, HALF, WIDE), F32),
            dma, dma((NQ,)), dma((2,)), *[dma((NQ, 2))] * 4,
            dma((4, 4)), dma((4, 4)), dma((4,)), dma, dma((NC,)),
            dma, dma((NC, 2)), dma, dma((NC, 2)), dma, dma((2, 4)),
        ],
        compiler_params=pltpu.CompilerParams(
            collective_id=0, has_side_effects=True, vmem_limit_bytes=53 << 20),
        cost_estimate=pl.CostEstimate(flops=2 << 30, bytes_accessed=4 << 20, transcendentals=0),
    )(integrals, amplitudes, tile_cols)


def solution(mesh):
    return jax.shard_map(
        body,
        mesh=mesh,
        in_specs=(P("row", ("col", "rep")), P(("row", "rep"), "col"), P("row", None)),
        out_specs=P(("row", "rep"), "col"),
        check_vma=False,
    )
```

```python
import jax
import jax.numpy as jnp
from jax import lax
from jax.experimental import pallas as pl
from jax.experimental.pallas import tpu as pltpu
from jax.sharding import PartitionSpec as P

TILE = 128
MESH = pl.DeviceIdType.MESH
BF16 = jnp.bfloat16
F32 = jnp.float32

NQ = 8
HALF = 64
WIDE = 256
ORDER = ((0, 0), (1, 0), (0, 1), (1, 1), (2, 0), (2, 1), (0, 2), (1, 2),
         (0, 3), (1, 3), (2, 2), (2, 3), (3, 0), (3, 1), (3, 2), (3, 3))
NC = len(ORDER)
A_TICK = (2, 3, 5, 7, 9, 11, 14, 18)
I_TICK = (4, 8, 11, 15)
C_TICK = (8, 10, 12, 13, 16, 17, 19, 20, 21, 22, 23, 24, 25, 26, 27, 28)
AHEAD = 3
LAG_CORE = 1
LAG_Y1 = 4
LAG_Y2 = 8


def choose(j, tiles):
    low = jnp.where(j == 0, tiles[0], tiles[1])
    high = jnp.where(j == 2, tiles[2], tiles[3])
    return jnp.where(j < 2, low, high)


def kernel(integrals, amplitudes, cols_in, out,
           tile_cols, raw0, raw1, ints, a0, a1, a2, a3, a4, a5, a6, a7, keep, give, got, y1, y2, zgot,
           load_t, load_a, load_i, a_send, a_recv, af_send, af_recv,
           i_send, i_recv, if_send, c_send, c_recv,
           y1_send, y1_recv, y2_send, y2_recv, z_send, z_recv):
    x = lax.axis_index("row")
    zl = lax.axis_index("col")
    p = lax.axis_index("rep")
    zh = p // 8
    y = lax.rem(p // 2, 4)
    core = lax.rem(p, 2)
    z = zh * 4 + zl
    xr, xl = lax.rem(x + 1, 4), lax.rem(x + 3, 4)
    yr, yl, yo = lax.rem(y + 1, 4), lax.rem(y + 3, 4), lax.rem(y + 2, 4)

    def at_x(v):
        return (v, zl, p)

    def at_y(v):
        return (x, zl, zh * 8 + v * 2 + core)

    def at_z(v):
        v = lax.rem(v + 8, 8)
        return (x, lax.rem(v, 4), (v // 4) * 8 + y * 2 + core)

    other_core = (x, zl, zh * 8 + y * 2 + (1 - core))

    def remote(src, dst, send, recv, dev):
        return pltpu.make_async_remote_copy(
            src_ref=src, dst_ref=dst, send_sem=send, recv_sem=recv,
            device_id=dev, device_id_type=MESH)

    def half(m):
        return (1 - zh) * (1 - m) + zh * m

    raw = (raw0, raw1)
    amps = (a0, a1, a2, a3, a4, a5, a6, a7)

    def i_load(m):
        rows = pl.ds(pl.multiple_of(half(m) * 1024, 1024), 1024)
        return pltpu.make_async_copy(integrals.at[rows], raw[m], load_i.at[m])

    t_load = pltpu.make_async_copy(cols_in, tile_cols, load_t)
    t_load.start()
    for m in range(2):
        i_load(m).start()

    def a_load(q):
        cols = pl.ds(pl.multiple_of(q * TILE, TILE), TILE)
        return pltpu.make_async_copy(amplitudes.at[:, cols], amps[q].at[x], load_a.at[q])

    for q in range(NQ):
        a_load(q).start()

    barrier = pltpu.get_barrier_semaphore()
    partners = [at_x(xr), at_x(xl), at_y(yr), at_y(yl), at_z(z + 1), at_z(z - 1),
                at_z(z + 2), at_z(z - 2), at_z(z + 4), other_core]
    for dev in partners:
        pl.semaphore_signal(barrier, inc=1, device_id=dev, device_id_type=MESH)

    def pack(m):
        i_load(m).wait()
        group = zl * 16 + p
        for k in range(8):
            i = half(m) * 8 + k
            j = tile_cols[i, group] - group * 4
            rows = pl.ds(k * TILE, TILE)
            ints[zl, i] = choose(j, [raw[m][rows, pl.ds(n * TILE, TILE)] for n in range(4)])

    def i_copy(u, h, send, target):
        part = ints.at[h, pl.ds(half(u // 2) * 8, 8), pl.ds(u % 2 * HALF, HALF)]
        return remote(part, part, send, i_recv.at[u, h], at_z(zh * 4 + target))

    steps = ((0, 2), (1, -2), (2, 1), (3, -1))

    def i_own(u, wait):
        for s, d in steps:
            @pl.when((zl + d >= 0) & (zl + d < 4))
            def _():
                copy = i_copy(u, zl, i_send.at[u, s], zl + d)
                if wait:
                    copy.wait_send()
                else:
                    copy.start()

    def i_forward(u, wait):
        @pl.when((zl == 1) | (zl == 2))
        def _():
            h = jnp.where(zl == 2, 0, 3)
            copy = i_copy(u, h, if_send.at[u], jnp.where(zl == 2, 3, 0))
            if wait:
                copy.wait_send()
            else:
                copy.wait_recv()
                copy.start()

    def i_arrive(u):
        for d in range(1, 4):
            h = lax.rem(zl + d, 4)

            @pl.when(jnp.logical_not(((zl == 2) & (h == 0)) | ((zl == 1) & (h == 3))))
            def _():
                i_copy(u, h, if_send.at[u], zl).wait_recv()

    def a_own(q, d):
        part = amps[q].at[x]
        return remote(part, part, a_send.at[q, d], a_recv.at[q, d], at_x((xr, xl)[d]))

    def a_from(q, d):
        part = amps[q].at[(xl, xr)[d]]
        return remote(part, part, a_send.at[q, d], a_recv.at[q, d], at_x((xr, xl)[d]))

    def a_pass(q, d):
        part = amps[q].at[(xl, xr)[d], pl.ds(d * 256, 256)]
        return remote(part, part, af_send.at[q, d], af_recv.at[q, d], at_x((xr, xl)[d]))

    def a_passed(q, d):
        part = amps[q].at[lax.rem(x + 2, 4), pl.ds(d * 256, 256)]
        return remote(part, part, af_send.at[q, d], af_recv.at[q, d], at_x((xr, xl)[d]))

    def a_start(q):
        a_load(q).wait()
        for d in range(2):
            a_own(q, d).start()

    pl.semaphore_wait(barrier, len(partners))
    a_start(0)
    t_load.wait()
    pack(0)
    i_own(0, False)
    for q in range(1, AHEAD):
        a_start(q)
    i_own(1, False)
    pack(1)

    def product(c, u, pair, cc, dst):
        for yy in range(4):
            i = half(u // 2) * 8 + yy * 2 + cc
            rows = pl.ds(pl.multiple_of(lax.rem(u, 2) * HALF, HALF), HALF)
            lhs, rhs = [], []
            for h in range(4):
                group = h * 16 + p
                j = tile_cols[i, group] - group * 4
                lhs.append(ints[h, i, rows])
                rhs.append(jnp.concatenate(
                    [choose(j, [amps[q][h, pl.ds(n * TILE, TILE)] for n in range(4)])
                     for q in (pair * 2, pair * 2 + 1)], axis=1))
            dst[c, yy] = jnp.dot(jnp.concatenate(lhs, axis=1), jnp.concatenate(rhs, axis=0),
                                 preferred_element_type=F32)

    def core_copy(c):
        return remote(give.at[c], got.at[c], c_send, c_recv.at[c], other_core)

    def y1_copy(c, d):
        return remote(keep.at[c, yo, pl.ds(d * 32, 32)], y1.at[c, d], y1_send, y1_recv.at[c, d],
                      at_y((yr, yl)[d]))

    def y2_copy(c, d):
        return remote(keep.at[c, (yr, yl)[d]], y2.at[c, d], y2_send, y2_recv.at[c, d],
                      at_y((yr, yl)[d]))

    def z_copy(c, u, pair):
        return remote(keep.at[c, y], zgot.at[lax.rem(u, 2), pair], z_send,
                      z_recv.at[lax.rem(u, 2), pair], at_z(z + 4))

    def table(t, ticks, values, none):
        found = jnp.int32(none)
        for at, value in zip(ticks, values):
            found = jnp.where(t == at, value, found)
        return found

    def tick(t, carry):
        for q in range(NQ):
            @pl.when(t == A_TICK[q])
            def _():
                for d in range(2):
                    a_from(q, d).wait_recv()
                    a_pass(q, d).start()
                if q + AHEAD < NQ:
                    a_start(q + AHEAD)

        for u in range(4):
            @pl.when(t == I_TICK[u])
            def _():
                i_forward(u, False)
                if u + 2 < 4:
                    i_own(u + 2, False)

        c = table(t, C_TICK, range(NC), -1)
        pair = table(t, C_TICK, [o[1] for o in ORDER], -1)
        u = table(t, C_TICK, [o[0] for o in ORDER], 0)
        for w in range(4):
            @pl.when(t == C_TICK[min(i for i, o in enumerate(ORDER) if o[0] == w)])
            def _():
                i_arrive(w)

            @pl.when(t == C_TICK[min(i for i, o in enumerate(ORDER) if o[1] == w)])
            def _():
                for q in (w * 2, w * 2 + 1):
                    for d in range(2):
                        a_passed(q, d).wait_recv()

        for w in range(4):
            @pl.when(pair == w)
            def _():
                product(c, u, w, 1 - core, give)
                core_copy(c).start()
                product(c, u, w, core, keep)

        @pl.when(t == C_TICK[-1] + 2)
        def _():
            for n in range(4):
                i_own(n, True)
                i_forward(n, True)
            for d in range(2):
                for q in range(NQ):
                    a_own(q, d).wait_send()
                    a_pass(q, d).wait_send()
            remote(give, give, c_send, c_recv.at[0], other_core).wait_send()

        c1 = table(t - LAG_CORE, C_TICK, range(NC), -1)

        @pl.when(c1 >= 0)
        def _():
            core_copy(c1).wait_recv()
            keep[c1, yo] += got[c1, yo]
            for d in range(2):
                y1_copy(c1, d).start()
            for v in (yr, yl, y):
                keep[c1, v] += got[c1, v]

        c2 = table(t - LAG_Y1, C_TICK, range(NC), -1)

        @pl.when(c2 >= 0)
        def _():
            for d in range(2):
                y1_copy(c2, d).wait_recv()
                keep[c2, (yr, yl)[d], pl.ds(d * 32, 32)] += y1[c2, d]
                y2_copy(c2, d).start()

        c3 = table(t - LAG_Y2, C_TICK, range(NC), -1)
        pair3 = table(t - LAG_Y2, C_TICK, [o[1] for o in ORDER], 0)
        u3 = table(t - LAG_Y2, C_TICK, [o[0] for o in ORDER], 0)

        @pl.when(c3 >= 0)
        def _():
            for d in range(2):
                y2_copy(c3, d).wait_recv()

            @pl.when(u3 < 2)
            def _():
                keep[c3, y] += y2[c3, 0] + y2[c3, 1]
                z_copy(c3, u3, pair3).start()

            @pl.when(u3 >= 2)
            def _():
                z_copy(c3, u3, pair3).wait_recv()
                total = (keep[c3, y] + y2[c3, 0]) + (y2[c3, 1] + zgot[u3 - 2, pair3])
                out[pl.ds(pl.multiple_of((u3 - 2) * HALF, HALF), HALF),
                    pl.ds(pl.multiple_of(pair3 * WIDE, WIDE), WIDE)] = total.astype(BF16)

        return carry

    lax.fori_loop(0, C_TICK[-1] + LAG_Y2 + 1, tick, 0)

    for buf, sem in ((y1, y1_send), (y2, y2_send), (zgot, z_send)):
        remote(buf, buf, sem, c_recv.at[0], other_core).wait_send()


def body(integrals, amplitudes, tile_cols):
    dma = pltpu.SemaphoreType.DMA
    return pl.pallas_call(
        kernel,
        out_shape=jax.ShapeDtypeStruct((TILE, 1024), BF16),
        in_specs=[pl.BlockSpec(memory_space=pltpu.HBM)] * 3,
        out_specs=pl.BlockSpec(memory_space=pltpu.VMEM),
        scratch_shapes=[
            pltpu.SMEM((16, 64), jnp.int32),
            *[pltpu.VMEM((1024, 512), BF16)] * 2,
            pltpu.VMEM((4, 16, TILE, TILE), BF16),
            *[pltpu.VMEM((4, 512, TILE), BF16)] * NQ,
            *[pltpu.VMEM((NC, 4, HALF, WIDE), F32)] * 3,
            pltpu.VMEM((NC, 2, HALF // 2, WIDE), F32),
            pltpu.VMEM((NC, 2, HALF, WIDE), F32),
            pltpu.VMEM((2, 4, HALF, WIDE), F32),
            dma, dma((NQ,)), dma((2,)), *[dma((NQ, 2))] * 4,
            dma((4, 4)), dma((4, 4)), dma((4,)), dma, dma((NC,)),
            dma, dma((NC, 2)), dma, dma((NC, 2)), dma, dma((2, 4)),
        ],
        compiler_params=pltpu.CompilerParams(
            collective_id=0, has_side_effects=True, vmem_limit_bytes=53 << 20),
        cost_estimate=pl.CostEstimate(flops=2 << 30, bytes_accessed=4 << 20, transcendentals=0),
    )(integrals, amplitudes, tile_cols)


def solution(mesh):
    return jax.shard_map(
        body,
        mesh=mesh,
        in_specs=(P("row", ("col", "rep")), P(("row", "rep"), "col"), P("row", None)),
        out_specs=P(("row", "rep"), "col"),
        check_vma=False,
    )
```
